32 devices in a mesh: chan: 8 (over z, x), tile: 4 (over y, core).
Axes of the slice: x: 2, y: 2, z: 4, core: 2. Of those that a mesh axis runs over, the one named last changes fastest.
Arguments:
- voltages: bfloat16 [2, 1024, 5888], P(None, 'chan'), may hold values from -6 to 6
- taps: float32 [16, 256], replicated, may hold values from -0.09375 to 0.09375
- beam_weights: bfloat16 [2, 256, 64, 1024], P(None, 'chan'), may hold values from -0.1875 to 0.1875
- station_masks: int32 [64, 512], replicated, may hold values 0 or 1
- tile_pairs: int32 [36, 2], P('tile'), may hold values from 0 to 7, as said below
Outputs:
- visibilities: float32 [2, 256, 36, 128, 128], P(None, 'chan', 'tile')
- beams: bfloat16 [2, 64, 8, 256], P(None, 'tile', 'chan')
The draws below stay inside these ranges and needn't reach their ends.
Inputs may be any that keep to these rules, and one draw needn't show every extreme that they name: `tile_pairs`: each pair (r, s) with 0 <= s <= r < 8 stands in exactly one row, r in the first column and s in the second.
All inputs are finite; a program needn't handle non-finite values.
Results may differ from the reference program's by a relative error of at most 0.0049.
Values may be sent and summed in bfloat16 or wider, within the bound.
A program may use at most 128 MiB of HBM per device.

```python
import jax
import jax.numpy as jnp
import numpy as np
from jax import lax

INPUTS = 1024
STATIONS = 512
CH = 256
BEAMS = 64
TAPS = 16
TB = 128
FRAMES = 8
NBLK = 8
NLOWER = 36


def draw_tile_pairs(key, part):
    row_table, col_table = np.tril_indices(NBLK)
    order = jax.random.permutation(key, NLOWER)
    row_values = jnp.asarray(row_table, dtype=jnp.int32)[order]
    col_values = jnp.asarray(col_table, dtype=jnp.int32)[order]
    return jnp.stack([row_values, col_values], axis=1).astype(jnp.int32)


def with_ends(drawn, key, low, top_value):
    place = [jax.random.randint(jax.random.fold_in(key, axis), (), 0, length) for axis, length in enumerate(drawn.shape)]
    main_axis = drawn.shape.index(max(drawn.shape))
    neighbour = place[:main_axis] + [(place[main_axis] + 1) % drawn.shape[main_axis]] + place[main_axis + 1:]
    return drawn.at[tuple(place)].set(low).at[tuple(neighbour)].set(top_value)


def block_scale(key, shape, shards, low, top_value):
    gain, own = 1.0, jax.random.fold_in(key, 6)
    for dim, parts in shards:
        steps = jnp.exp(jax.random.uniform(jax.random.fold_in(own, dim), (parts,), jnp.float32, low / len(shards), top_value / len(shards)))
        gain = gain * jnp.repeat(steps, shape[dim] // parts).reshape([-1 if axis == dim else 1 for axis in range(len(shape))])
    return gain


def gaussian(key, dims, scale, most, pieces=(), held_as=jnp.bfloat16):
    entries = jax.random.normal(key, dims, jnp.float32) * scale
    if len(pieces) > 0:
        entries = block_scale(key, dims, pieces, -0.22, 0.18) * entries
    return jnp.clip(entries, min=-most, max=most).astype(held_as)


def setup_inputs(seed: int = 0) -> dict:
    seeds = jax.random.split(jax.random.key(seed), 6)
    return {
        "voltages": gaussian(seeds[0], (2, INPUTS, (FRAMES + TAPS - 1) * CH), 1.0, 6.0, ((1, 8),)),
        "taps": gaussian(seeds[1], (TAPS, CH), (TAPS * CH) ** -0.5, 0.09375, (), jnp.float32),
        "beam_weights": gaussian(seeds[2], (2, CH, BEAMS, INPUTS), INPUTS ** -0.5, 0.1875, ((1, 8),)),
        "station_masks": with_ends((jax.random.randint(seeds[3], (BEAMS, STATIONS), 0, 4) < 3).astype(jnp.int32), jax.random.fold_in(seeds[3], 1), 0, 1),
        "tile_pairs": draw_tile_pairs(jax.random.fold_in(seeds[5], 71), 0),
    }


def reference(voltages, taps, beam_weights, station_masks, tile_pairs):
    framed = voltages.astype(jnp.float32).reshape(2, INPUTS, FRAMES + TAPS - 1, CH)
    frames = jnp.zeros((2, INPUTS, FRAMES, CH), jnp.float32)
    for tap_index in range(TAPS):
        frames = frames + taps[tap_index] * framed[:, :, tap_index:tap_index + FRAMES, :]
    spectrum = jnp.fft.fft(frames[0] + 1j * frames[1], axis=-1)
    stacked_parts = jnp.stack([jnp.real(spectrum), jnp.imag(spectrum)])
    spectra = jnp.transpose(stacked_parts, (3, 0, 1, 2)).astype(jnp.bfloat16)

    def one_channel(channel_block):
        tile_rows = channel_block.astype(jnp.float32).reshape(2, NBLK, TB, FRAMES)
        left_rows = tile_rows[:, tile_pairs[:, 0]]
        right_rows = tile_rows[:, tile_pairs[:, 1]]
        rotated = jnp.stack([left_rows[1], -left_rows[0]])
        stacked = jnp.stack([left_rows, rotated])
        return jnp.einsum("orkaw,rkbw->okab", stacked, right_rows)

    correlated = lax.map(one_channel, spectra)
    visibilities = jnp.transpose(correlated, (1, 0, 2, 3, 4)) * (1.0 / FRAMES)
    live_inputs = jnp.broadcast_to(station_masks[:, :, None], (BEAMS, STATIONS, 2)).reshape(BEAMS, INPUTS)
    weights = beam_weights.astype(jnp.float32) * live_inputs.astype(jnp.float32)[None, None]
    products = jnp.einsum("scbi,crit->csrbt", weights, spectra.astype(jnp.float32))
    real_part = products[:, 0, 0] - products[:, 1, 1]
    imag_part = products[:, 0, 1] + products[:, 1, 0]
    beams = jnp.transpose(jnp.stack([real_part, imag_part]), (0, 2, 3, 1)).astype(jnp.bfloat16)
    return (visibilities, beams)
```

```python
import functools
import math

import jax
import jax.numpy as jnp
import numpy as np
from jax import lax
from jax.experimental import pallas as pl
from jax.experimental.pallas import tpu as pltpu
from jax.sharding import PartitionSpec as P

TB = 128
MESH = pl.DeviceIdType.MESH
TURN_KERNEL = False


def dft_table(channels):
    counter = np.arange(channels, dtype=np.int64)
    phases = 2.0 * math.pi / channels * (counter[:, None] * counter[None, :] % channels)
    cosine, sine = np.cos(phases), np.sin(phases)
    first_row = np.stack([cosine, sine], axis=1)
    second_row = np.stack([-sine, cosine], axis=1)
    return np.stack([first_row, second_row], axis=1).astype(np.float32)


def filterbank(voltages, taps, count):
    taps_count, channels = taps.shape
    in_dev = voltages.shape[1]
    framed = voltages.reshape(2, in_dev, count + taps_count - 1, channels)
    frames = jnp.zeros((2, in_dev, count, channels), jnp.float32)
    for p in range(taps_count):
        frames = frames + taps[p] * framed[:, :, p : p + count, :].astype(jnp.float32)
    spectra = jnp.einsum(
        "csrk,ritk->csti",
        jnp.asarray(dft_table(channels)),
        frames,
        precision=lax.Precision.HIGHEST,
        preferred_element_type=jnp.float32,
    )
    return spectra.astype(jnp.bfloat16)


def turn_kernel(n, tq, volts, taps_ref, hi_ref, lo_ref, out, send, s1, r1, s2, r2, s3, r3, s4, r4):
    me = lax.axis_index("chan")
    tile = lax.axis_index("tile")
    far = lax.rem(tile + 2, 4)
    near = tile + 1 - 2 * lax.rem(tile, 2)
    taps_count, channels = taps_ref.shape
    rows = out.shape[2] // tq
    width = out.shape[3]

    barrier = pltpu.get_barrier_semaphore()

    @pl.loop(1, n)
    def _(k):
        pl.semaphore_signal(
            barrier, inc=1, device_id=(lax.rem(me + k, n), tile), device_id_type=MESH
        )

    for t in (far, near):
        pl.semaphore_signal(barrier, inc=1, device_id=(me, t), device_id_type=MESH)

    for t in range(tq):
        parts = []
        for r in range(2):
            total = jnp.zeros((width, channels), jnp.float32)
            for p in range(taps_count):
                at = pl.multiple_of((tile * tq + t + p) * channels, channels)
                total = total + taps_ref[p : p + 1, :] * volts[r, :, pl.ds(at, channels)].astype(
                    jnp.float32
                )
            parts.append(total)
        frame = jnp.concatenate(parts, axis=1)
        high = frame.astype(jnp.bfloat16)
        low = (frame - high.astype(jnp.float32)).astype(jnp.bfloat16)

        def nt(a, b):
            return lax.dot_general(
                a, b, (((1,), (1,)), ((), ())), preferred_element_type=jnp.float32
            )

        got = nt(hi_ref[...], high) + nt(hi_ref[...], low) + nt(lo_ref[...], high)
        send[:, t * rows : (t + 1) * rows, :] = got.astype(jnp.bfloat16).reshape(n, rows, width)

    pl.semaphore_wait(barrier, n + 1)

    def first(k, src):
        d = lax.rem(me + k, n)
        return pltpu.make_async_remote_copy(
            src_ref=send.at[d],
            dst_ref=out.at[src, tile],
            send_sem=s1.at[d],
            recv_sem=r1.at[src],
            device_id=(d, tile),
            device_id_type=MESH,
        )

    def onward(j, block, peer, ss, rr):
        return pltpu.make_async_remote_copy(
            src_ref=out.at[j, block],
            dst_ref=out.at[j, block],
            send_sem=ss.at[j],
            recv_sem=rr.at[j],
            device_id=(me, peer),
            device_id_type=MESH,
        )

    @pl.loop(1, n)
    def _(k):
        first(k, me).start()

    out[me, tile] = send[me]

    @pl.loop(0, n)
    def _(k):
        j = lax.rem(me + n - k, n)

        @pl.when(k > 0)
        def _():
            first(1, j).wait_recv()

        onward(j, tile, far, s2, r2).start()
        onward(j, tile, near, s3, r3).start()

    @pl.loop(0, n)
    def _(k):
        j = lax.rem(me + n - k, n)
        onward(j, far, far, s2, r2).wait_recv()
        onward(j, far, near, s4, r4).start()

    @pl.loop(0, n)
    def _(k):
        j = lax.rem(me + n - k, n)
        other = lax.rem(near + 2, 4)
        onward(j, near, near, s3, r3).wait_recv()
        onward(j, other, near, s4, r4).wait_recv()
        onward(j, tile, far, s2, r2).wait_send()
        onward(j, tile, near, s3, r3).wait_send()
        onward(j, far, near, s4, r4).wait_send()

        @pl.when(k > 0)
        def _():
            first(k, me).wait_send()


def turn(voltages, taps, total_time):
    taps_count, channels = taps.shape
    n = lax.axis_size("chan")
    tiles = lax.axis_size("tile")
    width = voltages.shape[1]
    cd = channels // n
    tq = total_time // tiles
    table = dft_table(channels).reshape(n, cd, 2, 2 * channels)
    table = table.transpose(0, 2, 1, 3).reshape(n * 2 * cd, 2 * channels)
    high = table.astype(jnp.bfloat16)
    low = (table - high.astype(np.float32)).astype(jnp.bfloat16)
    rows = tq * 2 * cd
    sem = [pltpu.SemaphoreType.DMA((n,))] * 8
    got = pl.pallas_call(
        functools.partial(turn_kernel, n, tq),
        out_shape=jax.ShapeDtypeStruct((n, tiles, rows, width), jnp.bfloat16),
        in_specs=[pl.BlockSpec(memory_space=pltpu.VMEM)] * 4,
        out_specs=pl.BlockSpec(memory_space=pltpu.VMEM),
        scratch_shapes=[pltpu.VMEM((n, rows, width), jnp.bfloat16)] + sem,
        compiler_params=pltpu.CompilerParams(
            collective_id=0, has_side_effects=True, vmem_limit_bytes=40 * 2**20
        ),
    )(voltages, taps, jnp.asarray(high), jnp.asarray(low))
    got = got.reshape(n, tiles, tq, 2, cd, width).transpose(4, 3, 1, 2, 0, 5)
    return got.reshape(cd, 2 * total_time, n * width)


def beam_kernel(time, where, w_ref, mask_ref, x_ref, out):
    beams = mask_ref.shape[0]
    mask = mask_ref[...]
    for c in range(x_ref.shape[0]):
        x = x_ref[c]
        prod = []
        for s in range(2):
            w = w_ref[s, c] * mask
            prod.append(
                lax.dot_general(
                    w, x, (((1,), (1,)), ((), ())), preferred_element_type=jnp.float32
                )
            )
        out[c, 0] = prod[0][:, :time] - prod[1][:, time:]
        out[c, 1] = prod[0][:, time:] + prod[1][:, :time]


def beamform(x, beam_weights, station_masks, tile_index):
    cd, rows, inputs = x.shape
    tiles = lax.axis_size("tile")
    beams = station_masks.shape[0] // tiles
    own = lax.dynamic_slice_in_dim(station_masks, tile_index * beams, beams, 0)
    live = jnp.repeat(own, 2, axis=1).astype(jnp.bfloat16)
    step = math.gcd(cd, 8)
    return pl.pallas_call(
        functools.partial(beam_kernel, rows // 2),
        out_shape=jax.ShapeDtypeStruct((cd, 2, beams, rows // 2), jnp.float32),
        grid_spec=pltpu.PrefetchScalarGridSpec(
            num_scalar_prefetch=1,
            grid=(cd // step,),
            in_specs=[
                pl.BlockSpec((2, step, beams, inputs), lambda i, at: (0, i, at[0], 0)),
                pl.BlockSpec((beams, inputs), lambda i, at: (0, 0)),
                pl.BlockSpec((step, rows, inputs), lambda i, at: (i, 0, 0)),
            ],
            out_specs=pl.BlockSpec((step, 2, beams, rows // 2), lambda i, at: (i, 0, 0, 0)),
        ),
        compiler_params=pltpu.CompilerParams(vmem_limit_bytes=40 * 2**20),
    )(tile_index[None].astype(jnp.int32), beam_weights, live, x)


def correlate_kernel(scale, pairs, x_ref, y_ref, out):
    for c in range(x_ref.shape[0]):
        for n in range(out.shape[2]):
            u = pl.ds(pl.multiple_of(pairs[n, 0] * TB, TB), TB)
            v = pl.ds(pl.multiple_of(pairs[n, 1] * TB, TB), TB)
            right = jnp.concatenate([x_ref[c, :, v], y_ref[c, :, v]], axis=1)
            got = lax.dot_general(
                x_ref[c, :, u],
                right,
                (((0,), (0,)), ((), ())),
                preferred_element_type=jnp.float32,
            )
            got = got * scale
            out[0, c, n] = got[:, :TB]
            out[1, c, n] = got[:, TB:]


def correlate(x, tile_pairs):
    cd, rows, inputs = x.shape
    time = rows // 2
    listed = tile_pairs.shape[0]
    rotated = jnp.concatenate([-x[:, time:], x[:, :time]], axis=1)
    step = math.gcd(cd, 2)
    return pl.pallas_call(
        functools.partial(correlate_kernel, 1.0 / time),
        out_shape=jax.ShapeDtypeStruct((2, cd, listed, TB, TB), jnp.float32),
        grid=(cd // step,),
        in_specs=[
            pl.BlockSpec(memory_space=pltpu.SMEM),
            pl.BlockSpec((step, rows, inputs), lambda i: (i, 0, 0)),
            pl.BlockSpec((step, rows, inputs), lambda i: (i, 0, 0)),
        ],
        out_specs=pl.BlockSpec((2, step, listed, TB, TB), lambda i: (0, i, 0, 0, 0)),
        cost_estimate=pl.CostEstimate(
            flops=4 * cd * listed * rows * TB * TB,
            bytes_accessed=8 * cd * listed * TB * TB,
            transcendentals=0,
        ),
        compiler_params=pltpu.CompilerParams(vmem_limit_bytes=40 * 2**20),
    )(tile_pairs, x, rotated)


def on_device(voltages, taps, beam_weights, station_masks, tile_pairs):
    taps_count, channels = taps.shape
    n = lax.axis_size("chan")
    tiles = lax.axis_size("tile")
    total_time = voltages.shape[2] // channels - taps_count + 1
    tile_index = lax.axis_index("tile")
    cd = channels // n
    aligned = tiles == 4 and (2 * cd) % 16 == 0 and voltages.shape[1] % 128 == 0
    if TURN_KERNEL and aligned:
        x = turn(voltages, taps, total_time)
    else:
        spectra = filterbank(voltages, taps, total_time)
        turned = lax.all_to_all(spectra, "chan", split_axis=0, concat_axis=3, tiled=True)
        x = turned.reshape(cd, 2 * total_time, turned.shape[3])
    part = beamform(x, beam_weights, station_masks, tile_index)
    part = jnp.transpose(part, (1, 2, 3, 0)).astype(jnp.bfloat16)
    beams = lax.all_to_all(part, "chan", split_axis=2, concat_axis=3, tiled=True)
    visibility = correlate(x, tile_pairs)
    return (visibility, beams)


def solution(mesh):
    in_specs = (P(None, "chan", None), P(), P(None, "chan", None, None), P(), P("tile", None))
    out_specs = (P(None, "chan", "tile", None, None), P(None, "tile", "chan", None))
    return jax.shard_map(
        on_device, mesh=mesh, in_specs=in_specs, out_specs=out_specs, check_vma=False
    )
```

```python
import functools
import math

import jax
import jax.numpy as jnp
import numpy as np
from jax import lax
from jax.experimental import pallas as pl
from jax.experimental.pallas import tpu as pltpu
from jax.sharding import PartitionSpec as P

TB = 128
MESH = pl.DeviceIdType.MESH
TURN_KERNEL = True


def dft_table(channels):
    counter = np.arange(channels, dtype=np.int64)
    phases = 2.0 * math.pi / channels * (counter[:, None] * counter[None, :] % channels)
    cosine, sine = np.cos(phases), np.sin(phases)
    first_row = np.stack([cosine, sine], axis=1)
    second_row = np.stack([-sine, cosine], axis=1)
    return np.stack([first_row, second_row], axis=1).astype(np.float32)


def filterbank(voltages, taps, count):
    taps_count, channels = taps.shape
    in_dev = voltages.shape[1]
    framed = voltages.reshape(2, in_dev, count + taps_count - 1, channels)
    frames = jnp.zeros((2, in_dev, count, channels), jnp.float32)
    for p in range(taps_count):
        frames = frames + taps[p] * framed[:, :, p : p + count, :].astype(jnp.float32)
    spectra = jnp.einsum(
        "csrk,ritk->csti",
        jnp.asarray(dft_table(channels)),
        frames,
        precision=lax.Precision.HIGHEST,
        preferred_element_type=jnp.float32,
    )
    return spectra.astype(jnp.bfloat16)


def turn_kernel(n, tq, volts, taps_ref, hi_ref, lo_ref, out, send, s1, r1, s2, r2, s3, r3, s4, r4):
    me = lax.axis_index("chan")
    tile = lax.axis_index("tile")
    far = lax.rem(tile + 2, 4)
    near = tile + 1 - 2 * lax.rem(tile, 2)
    taps_count, channels = taps_ref.shape
    rows = out.shape[2] // tq
    width = out.shape[3]

    barrier = pltpu.get_barrier_semaphore()

    @pl.loop(1, n)
    def _(k):
        pl.semaphore_signal(
            barrier, inc=1, device_id=(lax.rem(me + k, n), tile), device_id_type=MESH
        )

    for t in (far, near):
        pl.semaphore_signal(barrier, inc=1, device_id=(me, t), device_id_type=MESH)

    for t in range(tq):
        parts = []
        for r in range(2):
            total = jnp.zeros((width, channels), jnp.float32)
            for p in range(taps_count):
                at = pl.multiple_of((tile * tq + t + p) * channels, channels)
                total = total + taps_ref[p : p + 1, :] * volts[r, :, pl.ds(at, channels)].astype(
                    jnp.float32
                )
            parts.append(total)
        frame = jnp.concatenate(parts, axis=1)
        high = frame.astype(jnp.bfloat16)
        low = (frame - high.astype(jnp.float32)).astype(jnp.bfloat16)

        def nt(a, b):
            return lax.dot_general(
                a, b, (((1,), (1,)), ((), ())), preferred_element_type=jnp.float32
            )

        got = nt(hi_ref[...], high) + nt(hi_ref[...], low) + nt(lo_ref[...], high)
        send[:, t * rows : (t + 1) * rows, :] = got.astype(jnp.bfloat16).reshape(n, rows, width)

    pl.semaphore_wait(barrier, n + 1)

    def first(k, src):
        d = lax.rem(me + k, n)
        return pltpu.make_async_remote_copy(
            src_ref=send.at[d],
            dst_ref=out.at[src, tile],
            send_sem=s1.at[d],
            recv_sem=r1.at[src],
            device_id=(d, tile),
            device_id_type=MESH,
        )

    def onward(j, block, peer, ss, rr):
        return pltpu.make_async_remote_copy(
            src_ref=out.at[j, block],
            dst_ref=out.at[j, block],
            send_sem=ss.at[j],
            recv_sem=rr.at[j],
            device_id=(me, peer),
            device_id_type=MESH,
        )

    @pl.loop(1, n)
    def _(k):
        first(k, me).start()

    out[me, tile] = send[me]

    @pl.loop(0, n)
    def _(k):
        j = lax.rem(me + n - k, n)

        @pl.when(k > 0)
        def _():
            first(1, j).wait_recv()

        onward(j, tile, far, s2, r2).start()
        onward(j, tile, near, s3, r3).start()

    @pl.loop(0, n)
    def _(k):
        j = lax.rem(me + n - k, n)
        onward(j, far, far, s2, r2).wait_recv()
        onward(j, far, near, s4, r4).start()

    @pl.loop(0, n)
    def _(k):
        j = lax.rem(me + n - k, n)
        other = lax.rem(near + 2, 4)
        onward(j, near, near, s3, r3).wait_recv()
        onward(j, other, near, s4, r4).wait_recv()
        onward(j, tile, far, s2, r2).wait_send()
        onward(j, tile, near, s3, r3).wait_send()
        onward(j, far, near, s4, r4).wait_send()

        @pl.when(k > 0)
        def _():
            first(k, me).wait_send()


def turn(voltages, taps, total_time):
    taps_count, channels = taps.shape
    n = lax.axis_size("chan")
    tiles = lax.axis_size("tile")
    width = voltages.shape[1]
    cd = channels // n
    tq = total_time // tiles
    table = dft_table(channels).reshape(n, cd, 2, 2 * channels)
    table = table.transpose(0, 2, 1, 3).reshape(n * 2 * cd, 2 * channels)
    high = table.astype(jnp.bfloat16)
    low = (table - high.astype(np.float32)).astype(jnp.bfloat16)
    rows = tq * 2 * cd
    sem = [pltpu.SemaphoreType.DMA((n,))] * 8
    got = pl.pallas_call(
        functools.partial(turn_kernel, n, tq),
        out_shape=jax.ShapeDtypeStruct((n, tiles, rows, width), jnp.bfloat16),
        in_specs=[pl.BlockSpec(memory_space=pltpu.VMEM)] * 4,
        out_specs=pl.BlockSpec(memory_space=pltpu.VMEM),
        scratch_shapes=[pltpu.VMEM((n, rows, width), jnp.bfloat16)] + sem,
        compiler_params=pltpu.CompilerParams(
            collective_id=0, has_side_effects=True, vmem_limit_bytes=40 * 2**20
        ),
    )(voltages, taps, jnp.asarray(high), jnp.asarray(low))
    got = got.reshape(n, tiles, tq, 2, cd, width).transpose(4, 3, 1, 2, 0, 5)
    return got.reshape(cd, 2 * total_time, n * width)


def beam_kernel(time, where, w_ref, mask_ref, x_ref, out):
    beams = mask_ref.shape[0]
    mask = mask_ref[...]
    for c in range(x_ref.shape[0]):
        x = x_ref[c]
        prod = []
        for s in range(2):
            w = w_ref[s, c] * mask
            prod.append(
                lax.dot_general(
                    w, x, (((1,), (1,)), ((), ())), preferred_element_type=jnp.float32
                )
            )
        out[c, 0] = prod[0][:, :time] - prod[1][:, time:]
        out[c, 1] = prod[0][:, time:] + prod[1][:, :time]


def beamform(x, beam_weights, station_masks, tile_index):
    cd, rows, inputs = x.shape
    tiles = lax.axis_size("tile")
    beams = station_masks.shape[0] // tiles
    own = lax.dynamic_slice_in_dim(station_masks, tile_index * beams, beams, 0)
    live = jnp.repeat(own, 2, axis=1).astype(jnp.bfloat16)
    step = math.gcd(cd, 8)
    return pl.pallas_call(
        functools.partial(beam_kernel, rows // 2),
        out_shape=jax.ShapeDtypeStruct((cd, 2, beams, rows // 2), jnp.float32),
        grid_spec=pltpu.PrefetchScalarGridSpec(
            num_scalar_prefetch=1,
            grid=(cd // step,),
            in_specs=[
                pl.BlockSpec((2, step, beams, inputs), lambda i, at: (0, i, at[0], 0)),
                pl.BlockSpec((beams, inputs), lambda i, at: (0, 0)),
                pl.BlockSpec((step, rows, inputs), lambda i, at: (i, 0, 0)),
            ],
            out_specs=pl.BlockSpec((step, 2, beams, rows // 2), lambda i, at: (i, 0, 0, 0)),
        ),
        compiler_params=pltpu.CompilerParams(vmem_limit_bytes=40 * 2**20),
    )(tile_index[None].astype(jnp.int32), beam_weights, live, x)


def correlate_kernel(scale, pairs, x_ref, y_ref, out):
    for c in range(x_ref.shape[0]):
        for n in range(out.shape[2]):
            u = pl.ds(pl.multiple_of(pairs[n, 0] * TB, TB), TB)
            v = pl.ds(pl.multiple_of(pairs[n, 1] * TB, TB), TB)
            right = jnp.concatenate([x_ref[c, :, v], y_ref[c, :, v]], axis=1)
            got = lax.dot_general(
                x_ref[c, :, u],
                right,
                (((0,), (0,)), ((), ())),
                preferred_element_type=jnp.float32,
            )
            got = got * scale
            out[0, c, n] = got[:, :TB]
            out[1, c, n] = got[:, TB:]


def correlate(x, tile_pairs):
    cd, rows, inputs = x.shape
    time = rows // 2
    listed = tile_pairs.shape[0]
    rotated = jnp.concatenate([-x[:, time:], x[:, :time]], axis=1)
    step = math.gcd(cd, 2)
    return pl.pallas_call(
        functools.partial(correlate_kernel, 1.0 / time),
        out_shape=jax.ShapeDtypeStruct((2, cd, listed, TB, TB), jnp.float32),
        grid=(cd // step,),
        in_specs=[
            pl.BlockSpec(memory_space=pltpu.SMEM),
            pl.BlockSpec((step, rows, inputs), lambda i: (i, 0, 0)),
            pl.BlockSpec((step, rows, inputs), lambda i: (i, 0, 0)),
        ],
        out_specs=pl.BlockSpec((2, step, listed, TB, TB), lambda i: (0, i, 0, 0, 0)),
        cost_estimate=pl.CostEstimate(
            flops=4 * cd * listed * rows * TB * TB,
            bytes_accessed=8 * cd * listed * TB * TB,
            transcendentals=0,
        ),
        compiler_params=pltpu.CompilerParams(vmem_limit_bytes=40 * 2**20),
    )(tile_pairs, x, rotated)


def on_device(voltages, taps, beam_weights, station_masks, tile_pairs):
    taps_count, channels = taps.shape
    n = lax.axis_size("chan")
    tiles = lax.axis_size("tile")
    total_time = voltages.shape[2] // channels - taps_count + 1
    tile_index = lax.axis_index("tile")
    cd = channels // n
    aligned = tiles == 4 and (2 * cd) % 16 == 0 and voltages.shape[1] % 128 == 0
    if TURN_KERNEL and aligned:
        x = turn(voltages, taps, total_time)
    else:
        spectra = filterbank(voltages, taps, total_time)
        turned = lax.all_to_all(spectra, "chan", split_axis=0, concat_axis=3, tiled=True)
        x = turned.reshape(cd, 2 * total_time, turned.shape[3])
    part = beamform(x, beam_weights, station_masks, tile_index)
    part = jnp.transpose(part, (1, 2, 3, 0)).astype(jnp.bfloat16)
    beams = lax.all_to_all(part, "chan", split_axis=2, concat_axis=3, tiled=True)
    visibility = correlate(x, tile_pairs)
    return (visibility, beams)


def solution(mesh):
    in_specs = (P(None, "chan", None), P(), P(None, "chan", None, None), P(), P("tile", None))
    out_specs = (P(None, "chan", "tile", None, None), P(None, "tile", "chan", None))
    return jax.shard_map(
        on_device, mesh=mesh, in_specs=in_specs, out_specs=out_specs, check_vma=False
    )
```

```python
import functools
import math

import jax
import jax.numpy as jnp
import numpy as np
from jax import lax
from jax.experimental import pallas as pl
from jax.experimental.pallas import tpu as pltpu
from jax.sharding import PartitionSpec as P

TB = 128
MESH = pl.DeviceIdType.MESH
TURN_KERNEL = True


def dft_table(channels):
    counter = np.arange(channels, dtype=np.int64)
    phases = 2.0 * math.pi / channels * (counter[:, None] * counter[None, :] % channels)
    cosine, sine = np.cos(phases), np.sin(phases)
    first_row = np.stack([cosine, sine], axis=1)
    second_row = np.stack([-sine, cosine], axis=1)
    return np.stack([first_row, second_row], axis=1).astype(np.float32)


def filterbank(voltages, taps, count):
    taps_count, channels = taps.shape
    in_dev = voltages.shape[1]
    framed = voltages.reshape(2, in_dev, count + taps_count - 1, channels)
    frames = jnp.zeros((2, in_dev, count, channels), jnp.float32)
    for p in range(taps_count):
        frames = frames + taps[p] * framed[:, :, p : p + count, :].astype(jnp.float32)
    spectra = jnp.einsum(
        "csrk,ritk->csti",
        jnp.asarray(dft_table(channels)),
        frames,
        precision=lax.Precision.HIGHEST,
        preferred_element_type=jnp.float32,
    )
    return spectra.astype(jnp.bfloat16)


def turn_kernel(n, tq, volts, taps_ref, hi_ref, lo_ref, out, send, s1, r1, s2, r2, s3, r3, s4, r4):
    me = lax.axis_index("chan")
    tile = lax.axis_index("tile")
    far = lax.rem(tile + 2, 4)
    near = tile + 1 - 2 * lax.rem(tile, 2)
    taps_count, channels = taps_ref.shape
    rows = out.shape[2] // tq
    width = out.shape[3]

    barrier = pltpu.get_barrier_semaphore()

    @pl.loop(1, n)
    def _(k):
        pl.semaphore_signal(
            barrier, inc=1, device_id=(lax.rem(me + k, n), tile), device_id_type=MESH
        )

    for t in (far, near):
        pl.semaphore_signal(barrier, inc=1, device_id=(me, t), device_id_type=MESH)

    for t in range(tq):
        parts = []
        for r in range(2):
            total = jnp.zeros((width, channels), jnp.float32)
            for p in range(taps_count):
                at = pl.multiple_of((tile * tq + t + p) * channels, channels)
                total = total + taps_ref[p : p + 1, :] * volts[r, :, pl.ds(at, channels)].astype(
                    jnp.float32
                )
            parts.append(total)
        frame = jnp.concatenate(parts, axis=1)
        high = frame.astype(jnp.bfloat16)
        low = (frame - high.astype(jnp.float32)).astype(jnp.bfloat16)

        def nt(a, b):
            return lax.dot_general(
                a, b, (((1,), (1,)), ((), ())), preferred_element_type=jnp.float32
            )

        got = nt(hi_ref[...], high) + nt(hi_ref[...], low) + nt(lo_ref[...], high)
        send[:, t * rows : (t + 1) * rows, :] = got.astype(jnp.bfloat16).reshape(n, rows, width)

    pl.semaphore_wait(barrier, n + 1)

    def first(k, src):
        d = lax.rem(me + k, n)
        return pltpu.make_async_remote_copy(
            src_ref=send.at[d],
            dst_ref=out.at[src, tile],
            send_sem=s1.at[d],
            recv_sem=r1.at[src],
            device_id=(d, tile),
            device_id_type=MESH,
        )

    def onward(j, block, peer, ss, rr):
        return pltpu.make_async_remote_copy(
            src_ref=out.at[j, block],
            dst_ref=out.at[j, block],
            send_sem=ss.at[j],
            recv_sem=rr.at[j],
            device_id=(me, peer),
            device_id_type=MESH,
        )

    @pl.loop(1, n)
    def _(k):
        first(k, me).start()

    out[me, tile] = send[me]

    @pl.loop(0, n)
    def _(k):
        j = lax.rem(me + n - k, n)

        @pl.when(k > 0)
        def _():
            first(1, j).wait_recv()

        onward(j, tile, far, s2, r2).start()
        onward(j, tile, near, s3, r3).start()

    @pl.loop(0, n)
    def _(k):
        j = lax.rem(me + n - k, n)
        onward(j, far, far, s2, r2).wait_recv()
        onward(j, far, near, s4, r4).start()

    @pl.loop(0, n)
    def _(k):
        j = lax.rem(me + n - k, n)
        other = lax.rem(near + 2, 4)
        onward(j, near, near, s3, r3).wait_recv()
        onward(j, other, near, s4, r4).wait_recv()
        onward(j, tile, far, s2, r2).wait_send()
        onward(j, tile, near, s3, r3).wait_send()
        onward(j, far, near, s4, r4).wait_send()

        @pl.when(k > 0)
        def _():
            first(k, me).wait_send()


def turn(voltages, taps, total_time):
    taps_count, channels = taps.shape
    n = lax.axis_size("chan")
    tiles = lax.axis_size("tile")
    width = voltages.shape[1]
    cd = channels // n
    tq = total_time // tiles
    table = dft_table(channels).reshape(n, cd, 2, 2 * channels)
    table = table.transpose(0, 2, 1, 3).reshape(n * 2 * cd, 2 * channels)
    high = table.astype(jnp.bfloat16)
    low = (table - high.astype(np.float32)).astype(jnp.bfloat16)
    rows = tq * 2 * cd
    sem = [pltpu.SemaphoreType.DMA((n,))] * 8
    got = pl.pallas_call(
        functools.partial(turn_kernel, n, tq),
        out_shape=jax.ShapeDtypeStruct((n, tiles, rows, width), jnp.bfloat16),
        in_specs=[pl.BlockSpec(memory_space=pltpu.VMEM)] * 4,
        out_specs=pl.BlockSpec(memory_space=pltpu.VMEM),
        scratch_shapes=[pltpu.VMEM((n, rows, width), jnp.bfloat16)] + sem,
        compiler_params=pltpu.CompilerParams(
            collective_id=0, has_side_effects=True, vmem_limit_bytes=40 * 2**20
        ),
    )(voltages, taps, jnp.asarray(high), jnp.asarray(low))
    got = got.reshape(n, tiles, tq, 2, cd, width).transpose(4, 3, 1, 2, 0, 5)
    return got.reshape(cd, 2 * total_time, n * width)


def beam_kernel(time, where, w_ref, mask_ref, x_ref, out):
    beams = mask_ref.shape[0]
    mask = mask_ref[...]
    for c in range(x_ref.shape[0]):
        x = x_ref[c]
        prod = []
        for s in range(2):
            w = w_ref[s, c] * mask
            prod.append(
                lax.dot_general(
                    w, x, (((1,), (1,)), ((), ())), preferred_element_type=jnp.float32
                )
            )
        out[c, 0] = prod[0][:, :time] - prod[1][:, time:]
        out[c, 1] = prod[0][:, time:] + prod[1][:, :time]


def beamform(x, beam_weights, station_masks, tile_index):
    cd, rows, inputs = x.shape
    tiles = lax.axis_size("tile")
    beams = station_masks.shape[0] // tiles
    own = lax.dynamic_slice_in_dim(station_masks, tile_index * beams, beams, 0)
    live = jnp.repeat(own, 2, axis=1).astype(jnp.bfloat16)
    step = math.gcd(cd, 8)
    return pl.pallas_call(
        functools.partial(beam_kernel, rows // 2),
        out_shape=jax.ShapeDtypeStruct((cd, 2, beams, rows // 2), jnp.float32),
        grid_spec=pltpu.PrefetchScalarGridSpec(
            num_scalar_prefetch=1,
            grid=(cd // step,),
            in_specs=[
                pl.BlockSpec((2, step, beams, inputs), lambda i, at: (0, i, at[0], 0)),
                pl.BlockSpec((beams, inputs), lambda i, at: (0, 0)),
                pl.BlockSpec((step, rows, inputs), lambda i, at: (i, 0, 0)),
            ],
            out_specs=pl.BlockSpec((step, 2, beams, rows // 2), lambda i, at: (i, 0, 0, 0)),
        ),
        compiler_params=pltpu.CompilerParams(vmem_limit_bytes=54 * 2**20),
    )(tile_index[None].astype(jnp.int32), beam_weights, live, x)


def correlate_kernel(time, pairs, x_ref, y_ref, out):
    exact = time & (time - 1) == 0
    scale = 1.0 / time
    for c in range(x_ref.shape[0]):
        sides = []
        for n in range(out.shape[2]):
            u = pl.ds(pl.multiple_of(pairs[n, 0] * TB, TB), TB)
            v = pl.ds(pl.multiple_of(pairs[n, 1] * TB, TB), TB)
            left = x_ref[c, :, u]
            if exact:
                left = left * jnp.asarray(scale, left.dtype)
            sides.append((left, jnp.concatenate([x_ref[c, :, v], y_ref[c, :, v]], axis=1)))
        for n, (left, right) in enumerate(sides):
            got = lax.dot_general(
                left, right, (((0,), (0,)), ((), ())), preferred_element_type=jnp.float32
            )
            if not exact:
                got = got * scale
            out[0, c, n] = got[:, :TB]
            out[1, c, n] = got[:, TB:]


def correlate(x, tile_pairs):
    cd, rows, inputs = x.shape
    time = rows // 2
    listed = tile_pairs.shape[0]
    rotated = jnp.concatenate([-x[:, time:], x[:, :time]], axis=1)
    step = math.gcd(cd, 2)
    return pl.pallas_call(
        functools.partial(correlate_kernel, time),
        out_shape=jax.ShapeDtypeStruct((2, cd, listed, TB, TB), jnp.float32),
        grid=(cd // step,),
        in_specs=[
            pl.BlockSpec(memory_space=pltpu.SMEM),
            pl.BlockSpec((step, rows, inputs), lambda i: (i, 0, 0)),
            pl.BlockSpec((step, rows, inputs), lambda i: (i, 0, 0)),
        ],
        out_specs=pl.BlockSpec((2, step, listed, TB, TB), lambda i: (0, i, 0, 0, 0)),
        cost_estimate=pl.CostEstimate(
            flops=4 * cd * listed * rows * TB * TB,
            bytes_accessed=8 * cd * listed * TB * TB,
            transcendentals=0,
        ),
        compiler_params=pltpu.CompilerParams(vmem_limit_bytes=40 * 2**20),
    )(tile_pairs, x, rotated)


def on_device(voltages, taps, beam_weights, station_masks, tile_pairs):
    taps_count, channels = taps.shape
    n = lax.axis_size("chan")
    tiles = lax.axis_size("tile")
    total_time = voltages.shape[2] // channels - taps_count + 1
    tile_index = lax.axis_index("tile")
    cd = channels // n
    aligned = tiles == 4 and (2 * cd) % 16 == 0 and voltages.shape[1] % 128 == 0
    if TURN_KERNEL and aligned:
        x = turn(voltages, taps, total_time)
    else:
        spectra = filterbank(voltages, taps, total_time)
        turned = lax.all_to_all(spectra, "chan", split_axis=0, concat_axis=3, tiled=True)
        x = turned.reshape(cd, 2 * total_time, turned.shape[3])
    part = beamform(x, beam_weights, station_masks, tile_index)
    part = jnp.transpose(part, (1, 2, 3, 0)).astype(jnp.bfloat16)
    beams = lax.all_to_all(part, "chan", split_axis=2, concat_axis=3, tiled=True)
    visibility = correlate(x, tile_pairs)
    return (visibility, beams)


def solution(mesh):
    in_specs = (P(None, "chan", None), P(), P(None, "chan", None, None), P(), P("tile", None))
    out_specs = (P(None, "chan", "tile", None, None), P(None, "tile", "chan", None))
    return jax.shard_map(
        on_device, mesh=mesh, in_specs=in_specs, out_specs=out_specs, check_vma=False
    )
```

```python
import functools
import math

import jax
import jax.numpy as jnp
import numpy as np
from jax import lax
from jax.experimental import pallas as pl
from jax.experimental.pallas import tpu as pltpu
from jax.sharding import PartitionSpec as P

TB = 128
MESH = pl.DeviceIdType.MESH
TURN_KERNEL = True


def dft_table(channels):
    counter = np.arange(channels, dtype=np.int64)
    phases = 2.0 * math.pi / channels * (counter[:, None] * counter[None, :] % channels)
    cosine, sine = np.cos(phases), np.sin(phases)
    first_row = np.stack([cosine, sine], axis=1)
    second_row = np.stack([-sine, cosine], axis=1)
    return np.stack([first_row, second_row], axis=1).astype(np.float32)


def filterbank(voltages, taps, count):
    taps_count, channels = taps.shape
    in_dev = voltages.shape[1]
    framed = voltages.reshape(2, in_dev, count + taps_count - 1, channels)
    frames = jnp.zeros((2, in_dev, count, channels), jnp.float32)
    for p in range(taps_count):
        frames = frames + taps[p] * framed[:, :, p : p + count, :].astype(jnp.float32)
    spectra = jnp.einsum(
        "csrk,ritk->csti",
        jnp.asarray(dft_table(channels)),
        frames,
        precision=lax.Precision.HIGHEST,
        preferred_element_type=jnp.float32,
    )
    return spectra.astype(jnp.bfloat16)


def turn_kernel(n, tq, volts, taps_ref, hi_ref, lo_ref, out, send, s1, r1, s2, r2, s3, r3, s4, r4):
    me = lax.axis_index("chan")
    tile = lax.axis_index("tile")
    far = lax.rem(tile + 2, 4)
    near = tile + 1 - 2 * lax.rem(tile, 2)
    taps_count, channels = taps_ref.shape
    rows = out.shape[2] // tq
    width = out.shape[3]

    barrier = pltpu.get_barrier_semaphore()

    @pl.loop(1, n)
    def _(k):
        pl.semaphore_signal(
            barrier, inc=1, device_id=(lax.rem(me + k, n), tile), device_id_type=MESH
        )

    for t in (far, near):
        pl.semaphore_signal(barrier, inc=1, device_id=(me, t), device_id_type=MESH)

    for t in range(tq):
        parts = []
        for r in range(2):
            total = jnp.zeros((width, channels), jnp.float32)
            for p in range(taps_count):
                at = pl.multiple_of((tile * tq + t + p) * channels, channels)
                total = total + taps_ref[p : p + 1, :] * volts[r, :, pl.ds(at, channels)].astype(
                    jnp.float32
                )
            parts.append(total)
        frame = jnp.concatenate(parts, axis=1)
        high = frame.astype(jnp.bfloat16)
        low = (frame - high.astype(jnp.float32)).astype(jnp.bfloat16)

        def nt(a, b):
            return lax.dot_general(
                a, b, (((1,), (1,)), ((), ())), preferred_element_type=jnp.float32
            )

        got = nt(hi_ref[...], high) + nt(hi_ref[...], low) + nt(lo_ref[...], high)
        send[:, t * rows : (t + 1) * rows, :] = got.astype(jnp.bfloat16).reshape(n, rows, width)

    pl.semaphore_wait(barrier, n + 1)

    def first(k, src):
        d = lax.rem(me + k, n)
        return pltpu.make_async_remote_copy(
            src_ref=send.at[d],
            dst_ref=out.at[src, tile],
            send_sem=s1.at[d],
            recv_sem=r1.at[src],
            device_id=(d, tile),
            device_id_type=MESH,
        )

    def onward(j, block, peer, ss, rr):
        return pltpu.make_async_remote_copy(
            src_ref=out.at[j, block],
            dst_ref=out.at[j, block],
            send_sem=ss.at[j],
            recv_sem=rr.at[j],
            device_id=(me, peer),
            device_id_type=MESH,
        )

    @pl.loop(1, n)
    def _(k):
        first(k, me).start()

    out[me, tile] = send[me]

    @pl.loop(0, n)
    def _(k):
        j = lax.rem(me + n - k, n)

        @pl.when(k > 0)
        def _():
            first(1, j).wait_recv()

        onward(j, tile, far, s2, r2).start()
        onward(j, tile, near, s3, r3).start()

    @pl.loop(0, n)
    def _(k):
        j = lax.rem(me + n - k, n)
        onward(j, far, far, s2, r2).wait_recv()
        onward(j, far, near, s4, r4).start()

    @pl.loop(0, n)
    def _(k):
        j = lax.rem(me + n - k, n)
        other = lax.rem(near + 2, 4)
        onward(j, near, near, s3, r3).wait_recv()
        onward(j, other, near, s4, r4).wait_recv()
        onward(j, tile, far, s2, r2).wait_send()
        onward(j, tile, near, s3, r3).wait_send()
        onward(j, far, near, s4, r4).wait_send()

        @pl.when(k > 0)
        def _():
            first(k, me).wait_send()


def turn(voltages, taps, total_time):
    taps_count, channels = taps.shape
    n = lax.axis_size("chan")
    tiles = lax.axis_size("tile")
    width = voltages.shape[1]
    cd = channels // n
    tq = total_time // tiles
    table = dft_table(channels).reshape(n, cd, 2, 2 * channels)
    table = table.transpose(0, 2, 1, 3).reshape(n * 2 * cd, 2 * channels)
    high = table.astype(jnp.bfloat16)
    low = (table - high.astype(np.float32)).astype(jnp.bfloat16)
    rows = tq * 2 * cd
    sem = [pltpu.SemaphoreType.DMA((n,))] * 8
    got = pl.pallas_call(
        functools.partial(turn_kernel, n, tq),
        out_shape=jax.ShapeDtypeStruct((n, tiles, rows, width), jnp.bfloat16),
        in_specs=[pl.BlockSpec(memory_space=pltpu.VMEM)] * 4,
        out_specs=pl.BlockSpec(memory_space=pltpu.VMEM),
        scratch_shapes=[pltpu.VMEM((n, rows, width), jnp.bfloat16)] + sem,
        compiler_params=pltpu.CompilerParams(
            collective_id=0, has_side_effects=True, vmem_limit_bytes=40 * 2**20
        ),
    )(voltages, taps, jnp.asarray(high), jnp.asarray(low))
    got = got.reshape(n, tiles, tq, 2, cd, width).transpose(4, 3, 1, 2, 0, 5)
    return got.reshape(cd, 2 * total_time, n * width)


def beam_kernel(time, where, w_ref, mask_ref, x_ref, out):
    beams = mask_ref.shape[0]
    mask = mask_ref[...]
    for c in range(x_ref.shape[0]):
        x = x_ref[c]
        prod = []
        for s in range(2):
            w = w_ref[s, c] * mask
            prod.append(
                lax.dot_general(
                    w, x, (((1,), (1,)), ((), ())), preferred_element_type=jnp.float32
                )
            )
        out[c, 0] = prod[0][:, :time] - prod[1][:, time:]
        out[c, 1] = prod[0][:, time:] + prod[1][:, :time]


def beamform(x, beam_weights, station_masks, tile_index):
    cd, rows, inputs = x.shape
    tiles = lax.axis_size("tile")
    beams = station_masks.shape[0] // tiles
    own = lax.dynamic_slice_in_dim(station_masks, tile_index * beams, beams, 0)
    live = jnp.repeat(own, 2, axis=1).astype(jnp.bfloat16)
    step = math.gcd(cd, 8)
    return pl.pallas_call(
        functools.partial(beam_kernel, rows // 2),
        out_shape=jax.ShapeDtypeStruct((cd, 2, beams, rows // 2), jnp.float32),
        grid_spec=pltpu.PrefetchScalarGridSpec(
            num_scalar_prefetch=1,
            grid=(cd // step,),
            in_specs=[
                pl.BlockSpec((2, step, beams, inputs), lambda i, at: (0, i, at[0], 0)),
                pl.BlockSpec((beams, inputs), lambda i, at: (0, 0)),
                pl.BlockSpec((step, rows, inputs), lambda i, at: (i, 0, 0)),
            ],
            out_specs=pl.BlockSpec((step, 2, beams, rows // 2), lambda i, at: (i, 0, 0, 0)),
        ),
        compiler_params=pltpu.CompilerParams(vmem_limit_bytes=40 * 2**20),
    )(tile_index[None].astype(jnp.int32), beam_weights, live, x)


def correlate_kernel(scale, pairs, x_ref, y_ref, out, held, sems):
    step = x_ref.shape[0]
    slots = held.shape[0]
    i = pl.program_id(0)
    last = pl.num_programs(0) - 1

    def send(at, o, c):
        slot = lax.rem(at, slots)
        return pltpu.make_async_copy(
            held.at[slot, o, c], out.at[o, at * step + c], sems.at[slot, o, c]
        )

    def finish(at):
        for c in range(step):
            for o in range(2):
                send(at, o, c).wait()

    @pl.when(i >= slots)
    def _():
        finish(i - slots)

    slot = lax.rem(i, slots)
    for c in range(step):
        for n in range(held.shape[3]):
            u = pl.ds(pl.multiple_of(pairs[n, 0] * TB, TB), TB)
            v = pl.ds(pl.multiple_of(pairs[n, 1] * TB, TB), TB)
            right = jnp.concatenate([x_ref[c, :, v], y_ref[c, :, v]], axis=1)
            got = lax.dot_general(
                x_ref[c, :, u],
                right,
                (((0,), (0,)), ((), ())),
                preferred_element_type=jnp.float32,
            )
            got = got * scale
            held[slot, 0, c, n] = got[:, :TB]
            held[slot, 1, c, n] = got[:, TB:]
        for o in range(2):
            send(i, o, c).start()

    @pl.when(i == last)
    def _():
        for back in range(slots - 1, -1, -1):
            finish(i - back)


def correlate(x, tile_pairs):
    cd, rows, inputs = x.shape
    time = rows // 2
    listed = tile_pairs.shape[0]
    rotated = jnp.concatenate([-x[:, time:], x[:, :time]], axis=1)
    step = math.gcd(cd, 2)
    slots = min(4, cd // step)
    return pl.pallas_call(
        functools.partial(correlate_kernel, 1.0 / time),
        out_shape=jax.ShapeDtypeStruct((2, cd, listed, TB, TB), jnp.float32),
        grid=(cd // step,),
        in_specs=[
            pl.BlockSpec(memory_space=pltpu.SMEM),
            pl.BlockSpec((step, rows, inputs), lambda i: (i, 0, 0)),
            pl.BlockSpec((step, rows, inputs), lambda i: (i, 0, 0)),
        ],
        out_specs=pl.BlockSpec(memory_space=pl.ANY),
        scratch_shapes=[
            pltpu.VMEM((slots, 2, step, listed, TB, TB), jnp.float32),
            pltpu.SemaphoreType.DMA((slots, 2, step)),
        ],
        cost_estimate=pl.CostEstimate(
            flops=4 * cd * listed * rows * TB * TB,
            bytes_accessed=8 * cd * listed * TB * TB,
            transcendentals=0,
        ),
        compiler_params=pltpu.CompilerParams(vmem_limit_bytes=40 * 2**20),
    )(tile_pairs, x, rotated)


def on_device(voltages, taps, beam_weights, station_masks, tile_pairs):
    taps_count, channels = taps.shape
    n = lax.axis_size("chan")
    tiles = lax.axis_size("tile")
    total_time = voltages.shape[2] // channels - taps_count + 1
    tile_index = lax.axis_index("tile")
    cd = channels // n
    aligned = tiles == 4 and (2 * cd) % 16 == 0 and voltages.shape[1] % 128 == 0
    if TURN_KERNEL and aligned:
        x = turn(voltages, taps, total_time)
    else:
        spectra = filterbank(voltages, taps, total_time)
        turned = lax.all_to_all(spectra, "chan", split_axis=0, concat_axis=3, tiled=True)
        x = turned.reshape(cd, 2 * total_time, turned.shape[3])
    part = beamform(x, beam_weights, station_masks, tile_index)
    part = jnp.transpose(part, (1, 2, 3, 0)).astype(jnp.bfloat16)
    beams = lax.all_to_all(part, "chan", split_axis=2, concat_axis=3, tiled=True)
    visibility = correlate(x, tile_pairs)
    return (visibility, beams)


def solution(mesh):
    in_specs = (P(None, "chan", None), P(), P(None, "chan", None, None), P(), P("tile", None))
    out_specs = (P(None, "chan", "tile", None, None), P(None, "tile", "chan", None))
    return jax.shard_map(
        on_device, mesh=mesh, in_specs=in_specs, out_specs=out_specs, check_vma=False
    )
```
